256 devices in a mesh: row: 16 (over x, y_lo, core), col: 16 (over y_hi, z).
Axes of the slice: x: 4, y: 4 (y_hi: 2, y_lo: 2; y = y_hi * 2 + y_lo), z: 8, core: 2. Of those that a mesh axis runs over, the one named last changes fastest.
Arguments:
- start_block: float32 [64, 65536], P(None, ('col', 'row')), may hold values from -6 to 6
- tile_values: bfloat16 [16, 16, 80, 256, 256], P('row', 'col'), may hold values from 0.0001 to 1
- tile_rows: int32 [16, 16, 80], P('row', 'col'), may hold values from 0 to 15, as said below
- tile_cols: int32 [16, 16, 80], P('row', 'col'), may hold values from 0 to 15, as said below
- tile_count: int32 [16, 16], P('row', 'col'), may hold values from 16 to 80, as said below
Outputs:
- filtered: float32 [64, 65536], P(None, ('col', 'row'))
- preceding: float32 [64, 65536], P(None, ('col', 'row'))
The draws below stay inside these ranges and needn't reach their ends.
Inputs may be any that keep to these rules, and one draw needn't show every extreme that they name: `tile_count`: the busiest device has exactly 80 live slots. `tile_rows`: slot k below max(16, 16) lies at tile row k % 16; slots at the same coordinates add. `tile_cols`: slot k below max(16, 16) lies at tile column k % 16.
All inputs are finite; a program needn't handle non-finite values.
Results may differ from the reference program's by a relative error of at most 0.0028.
Values may be sent and summed in bfloat16 or wider, within the bound.
No kernel may reach another device: no remote copies, remote signals or barrier semaphores. Data moves between devices by JAX's collectives and lax.ppermute only.
A program may use at most 64 MiB of HBM per device.

```python
import jax
import jax.numpy as jnp
from jax import lax

TILE = 256
COLS = 64
DEGREE = 3
TR_DEV = 16
TC_DEV = 16
TILES_DEV = 80
NODES = 65536
N_ROW = 16
N_COL = 16


def draw_tile_values(key, part):
    key = jax.random.fold_in(key, 14)
    sharpness = TILE * N_COL / 4.0

    def one_device(index):
        device_key = jax.random.fold_in(key, index)
        keys = jax.random.split(device_key, 1)
        spread = jax.random.uniform(keys[0], (TILES_DEV, TILE, TILE), jnp.float32)
        heavy = jnp.exp(-sharpness * spread)
        return (heavy + 0.0001).astype(jnp.bfloat16)
    flat_tiles = lax.map(one_device, jnp.arange(N_ROW * N_COL, dtype=jnp.int32))
    return flat_tiles.reshape(N_ROW, N_COL, TILES_DEV, TILE, TILE)


def draw_tile_rows(key, part):
    key = jax.random.fold_in(key, 11)
    cover = max(TR_DEV, TC_DEV)
    slot_index = jnp.arange(TILES_DEV, dtype=jnp.int32)
    random_rows = jax.random.randint(key, (N_ROW, N_COL, TILES_DEV), 0, TR_DEV, dtype=jnp.int32)
    return jnp.where(slot_index < cover, slot_index % TR_DEV, random_rows).astype(jnp.int32)


def draw_tile_cols(key, part):
    key = jax.random.fold_in(key, 12)
    cover = max(TR_DEV, TC_DEV)
    slot_index = jnp.arange(TILES_DEV, dtype=jnp.int32)
    random_cols = jax.random.randint(key, (N_ROW, N_COL, TILES_DEV), 0, TC_DEV, dtype=jnp.int32)
    return jnp.where(slot_index < cover, slot_index % TC_DEV, random_cols).astype(jnp.int32)


def draw_tile_count(key, part):
    key = jax.random.fold_in(key, 13)
    keys = jax.random.split(key, 4)
    cover = max(TR_DEV, TC_DEV)
    spare = TILES_DEV - cover
    first = jax.random.randint(keys[0], (N_ROW, N_COL), 0, spare + 1, dtype=jnp.int32)
    second = jax.random.randint(keys[1], (N_ROW, N_COL), 0, spare + 1, dtype=jnp.int32)
    third = jax.random.randint(keys[2], (N_ROW, N_COL), 0, spare + 1, dtype=jnp.int32)
    extra = jnp.minimum(jnp.minimum(first, second), third)
    chosen = jax.random.randint(keys[3], (), 0, N_ROW * N_COL, dtype=jnp.int32)
    flat_counts = (cover + extra).reshape(N_ROW * N_COL)
    flat_counts = jnp.where(jnp.arange(N_ROW * N_COL, dtype=jnp.int32) == chosen, TILES_DEV, flat_counts)
    return flat_counts.reshape(N_ROW, N_COL).astype(jnp.int32)


def shard_levels(rng, dims, cuts, smallest, high):
    level = 1.0
    for dim, blocks in cuts:
        draws = jax.random.uniform(jax.random.fold_in(jax.random.fold_in(rng, 6), dim), (blocks,), jnp.float32, smallest / len(cuts), high / len(cuts))
        level = level * jnp.repeat(jnp.exp(draws), dims[dim] // blocks).reshape((-1,) + (1,) * (len(dims) - 1 - dim))
    return level


def scatter_about(own_key, dims, deviation, most, shards=(), kind=jnp.bfloat16):
    factor_of = shard_levels(own_key, dims, shards, -0.22, 0.18) if shards else 1.0
    result = jax.random.normal(own_key, dims, jnp.float32) * deviation * factor_of
    return jnp.minimum(jnp.maximum(result, -most), most).astype(kind)


def setup_inputs(seed: int = 0) -> dict:
    arg_keys = jax.random.split(jax.random.key(seed), 6)
    return {
        "start_block": scatter_about(arg_keys[0], (COLS, NODES), 1.0, 6.0, ((1, 256),), jnp.float32),
        "tile_values": draw_tile_values(jax.random.fold_in(arg_keys[5], 71), 0),
        "tile_rows": draw_tile_rows(jax.random.fold_in(arg_keys[5], 71), 0),
        "tile_cols": draw_tile_cols(jax.random.fold_in(arg_keys[5], 71), 0),
        "tile_count": draw_tile_count(jax.random.fold_in(arg_keys[5], 71), 0),
    }


filter_center = 0.4
filter_half = 0.4

def coordinates(tile_rows, tile_cols, tile_count):
    slot_index = jnp.arange(TILES_DEV, dtype=jnp.int32)
    row_base = (jnp.arange(N_ROW, dtype=jnp.int32) * TR_DEV)[:, None, None]
    col_base = (jnp.arange(N_COL, dtype=jnp.int32) * TC_DEV)[None, :, None]
    global_rows = (tile_rows + row_base).astype(jnp.int32).reshape(N_ROW * N_COL, TILES_DEV)
    global_cols = (tile_cols + col_base).astype(jnp.int32).reshape(N_ROW * N_COL, TILES_DEV)
    live_mask = (slot_index[None, None, :] < tile_count[:, :, None]).astype(jnp.float32)
    return (global_rows, global_cols, live_mask.reshape(N_ROW * N_COL, TILES_DEV))

def spread_tiles(source, flat_values, take_all, put_all, live_mask, transposed):

    def advance(running, item):
        values, take_index, put_index, mask_row = item
        gathered = jnp.take(source, take_index, axis=1)
        dense = values.astype(jnp.float32)
        if transposed:
            contrib = jnp.einsum('cki,kij->ckj', gathered, dense, precision=lax.Precision.HIGHEST)
        else:
            contrib = jnp.einsum('ckj,kij->cki', gathered, dense, precision=lax.Precision.HIGHEST)
        contrib = contrib * mask_row[None, :, None]
        return (running.at[:, put_index].add(contrib), None)
    start_sum = jnp.zeros(source.shape, jnp.float32)
    running, _ = lax.scan(advance, start_sum, (flat_values, take_all, put_all, live_mask))
    return running

def degree_sums(flat_values, put_all, live_mask, axis_sum):

    def advance(running, item):
        values, put_index, mask_row = item
        sums = lax.optimization_barrier(jnp.sum(values.astype(jnp.float32), axis=axis_sum)) * mask_row[:, None]
        return (running.at[put_index].add(sums), None)
    start_sum = jnp.zeros((NODES // TILE, TILE), jnp.float32)
    running, _ = lax.scan(advance, start_sum, (flat_values, put_all, live_mask))
    return running.reshape(NODES)

def reference(start_block, tile_values, tile_rows, tile_cols, tile_count):
    tile_total = NODES // TILE
    global_rows, global_cols, live_mask = coordinates(tile_rows, tile_cols, tile_count)
    flat_values = tile_values.reshape(N_ROW * N_COL, TILES_DEV, TILE, TILE)
    row_degree = degree_sums(flat_values, global_rows, live_mask, 2)
    col_degree = degree_sums(flat_values, global_cols, live_mask, 1)
    col_scale = lax.rsqrt(col_degree)
    row_inverse = 1.0 / row_degree

    def apply_filter(vector):
        scaled = lax.optimization_barrier((col_scale * vector).astype(jnp.bfloat16)).astype(jnp.float32)
        mixed = spread_tiles(scaled.reshape(COLS, tile_total, TILE), flat_values, global_cols, global_rows, live_mask, False)
        mixed = mixed.reshape(COLS, NODES)
        weighted = lax.optimization_barrier((mixed * row_inverse).astype(jnp.bfloat16)).astype(jnp.float32)
        back = spread_tiles(weighted.reshape(COLS, tile_total, TILE), flat_values, global_rows, global_cols, live_mask, True)
        back = back.reshape(COLS, NODES)
        return (col_scale * back - filter_center * vector) / filter_half
    previous = start_block
    current = apply_filter(start_block)
    for step_index in range(DEGREE - 1):
        previous, current = (current, 2.0 * apply_filter(current) - previous)
    return (current, previous)
```

```python
import functools

import jax
import jax.numpy as jnp
from jax import lax
from jax.experimental import pallas as pl
from jax.experimental.pallas import tpu as pltpu
from jax.sharding import PartitionSpec as P

DEGREE = 3
GROUP = 8

filter_center = 0.4
filter_half = 0.4

bf16, f32 = jnp.bfloat16, jnp.float32


def split_sums(sums):
    place = lax.broadcasted_iota(jnp.int32, sums.shape, 0)
    high = sums.astype(bf16).astype(f32)
    middle = (sums - high).astype(bf16).astype(f32)
    low = sums - high - middle
    return jnp.where(place == 0, high, jnp.where(place == 1, middle, jnp.where(place == 2, low, 0.0)))


def spread_kernel(transposed, degree_rows, count_ref, take_ref, put_ref, source_ref, tiles_ref, out_ref, total_ref):
    cover = total_ref.shape[0]
    slots = tiles_ref.shape[0]
    count = count_ref[0, 0]
    contract = (((1,), (1 if transposed else 0,)), ((), ()))

    def product(slot, take):
        return lax.dot_general(source_ref[take], tiles_ref[slot], contract, preferred_element_type=f32)

    for slot in range(cover):
        total_ref[slot] = product(slot, slot)

    def step(index, carry):
        first = cover + index * GROUP
        places, terms = [], []
        for offset in range(GROUP):
            slot = jnp.minimum(first + offset, slots - 1)
            term = product(slot, take_ref[0, slot])
            places.append(put_ref[0, slot])
            terms.append(jnp.where(first + offset < count, term, 0.0))
        for place, term in zip(places, terms):
            total_ref[place] += term
        return carry

    lax.fori_loop(0, (count - cover + GROUP - 1) // GROUP, step, 0)
    if degree_rows:
        vectors = total_ref.shape[1] - degree_rows
        out_ref[:, :vectors] = total_ref[:, :vectors].astype(out_ref.dtype)
        for place in range(cover):
            out_ref[place, vectors:] = split_sums(total_ref[place, vectors:]).astype(out_ref.dtype)
    else:
        out_ref[...] = total_ref[...].astype(out_ref.dtype)


def spread_tiles(source, tiles, take, put, count, transposed, dtype=bf16, degree_rows=0):
    smem = pl.BlockSpec(memory_space=pltpu.SMEM)
    vmem = pl.BlockSpec(memory_space=pltpu.VMEM)
    flops = 2 * tiles.size * source.shape[1]
    return pl.pallas_call(
        functools.partial(spread_kernel, transposed, degree_rows),
        out_shape=jax.ShapeDtypeStruct(source.shape, dtype),
        in_specs=[smem, smem, smem, vmem, vmem],
        out_specs=vmem,
        scratch_shapes=[pltpu.VMEM(source.shape, f32)],
        compiler_params=pltpu.CompilerParams(vmem_limit_bytes=16 * 2**20),
        cost_estimate=pl.CostEstimate(flops=flops, bytes_accessed=source.size * 4, transcendentals=0),
    )(count, take, put, source, tiles)


def on_device(start_block, tile_values, tile_rows, tile_cols, tile_count):
    vectors, piece = start_block.shape
    tiles = pltpu.with_memory_space_constraint(tile_values[0, 0], pltpu.VMEM)
    rows, cols = tile_rows[0], tile_cols[0]
    row_parts, col_parts = lax.axis_size("col"), lax.axis_size("row")

    def to_all(block, axis, parts):
        return lax.all_to_all(jnp.broadcast_to(block[None], (parts, *block.shape)), axis, 0, 0)

    def sum_parts(parts, axis):
        return jnp.sum(lax.all_to_all(parts, axis, 0, 0).astype(f32), axis=0)

    ones = jnp.ones((row_parts, 16, piece), bf16)
    col_terms = spread_tiles(ones, tiles, rows, cols, tile_count, False, dtype=f32)
    col_degree = sum_parts(col_terms[:, :8], "row")[0]
    col_scale = lax.rsqrt(col_degree)

    def forward(scaled, row_inverse):
        gathered = to_all(scaled, "row", col_parts)
        if row_inverse is None:
            gathered = jnp.concatenate([gathered, jnp.ones((col_parts, 16, piece), bf16)], axis=1)
            mixed = spread_tiles(gathered, tiles, cols, rows, tile_count, True, degree_rows=16)
            mixed = sum_parts(mixed, "col")
            row_inverse = 1.0 / (mixed[vectors] + mixed[vectors + 1] + mixed[vectors + 2])
            return mixed[:vectors], row_inverse
        mixed = spread_tiles(gathered, tiles, cols, rows, tile_count, True)
        return sum_parts(mixed, "col"), row_inverse

    def backward(weighted):
        gathered = to_all(weighted, "col", row_parts)
        return sum_parts(spread_tiles(gathered, tiles, rows, cols, tile_count, False), "row")

    def apply_filter(vector, row_inverse):
        scaled = (col_scale * vector).astype(bf16)
        mixed, row_inverse = forward(scaled, row_inverse)
        weighted = (mixed * row_inverse).astype(bf16)
        back = backward(weighted)
        return (col_scale * back - filter_center * vector) / filter_half, row_inverse

    previous = start_block
    current, row_inverse = apply_filter(start_block, None)
    for _ in range(DEGREE - 1):
        following, row_inverse = apply_filter(current, row_inverse)
        previous, current = current, 2.0 * following - previous
    return current, previous


def solution(mesh):
    return jax.shard_map(
        on_device,
        mesh=mesh,
        in_specs=(
            P(None, ("col", "row")),
            P("row", "col", None, None, None),
            P("row", "col", None),
            P("row", "col", None),
            P("row", "col"),
        ),
        out_specs=(P(None, ("col", "row")), P(None, ("col", "row"))),
        check_vma=False,
    )
```

```python
import functools
import math

import jax
import jax.numpy as jnp
from jax import lax
from jax.experimental import pallas as pl
from jax.experimental.pallas import tpu as pltpu
from jax.sharding import PartitionSpec as P

DEGREE = 3
GROUP = 16
LOAD = 8
AHEAD = 6
EXTRA = 8
FINE = 512.0

filter_center = 0.4
filter_half = 0.4

f16, bf16, f32 = jnp.float16, jnp.bfloat16, jnp.float32
SMEM = pl.BlockSpec(memory_space=pltpu.SMEM)
VMEM = pl.BlockSpec(memory_space=pltpu.VMEM)
HBM = pl.BlockSpec(memory_space=pltpu.HBM)


def halves_of(sums):
    high = sums.astype(bf16).astype(f32)
    return high, (sums - high) * FINE


def load_kernel(
    count_in, rows_in, cols_in, start_in, tiles_ref, held_ref, sent_ref, count_ref, rows_ref, cols_ref,
    start_ref, total_ref, done, read,
):
    slots, width = tiles_ref.shape[0], tiles_ref.shape[2]
    vectors, cover = start_ref.shape[0], total_ref.shape[0]
    pairs = ((start_in, start_ref), (count_in, count_ref), (cols_in, cols_ref), (rows_in, rows_ref))
    small = [pltpu.make_async_copy(*pair, read.at[place]) for place, pair in enumerate(pairs)]
    large = [
        pltpu.make_async_copy(tiles_ref.at[pl.ds(first, LOAD)], held_ref.at[pl.ds(first, LOAD)], done.at[place])
        for place, first in enumerate(range(0, slots, LOAD))
    ]
    for copy in small + large[:AHEAD]:
        copy.start()
    for copy in small:
        copy.wait()
    count = count_ref[0, 0]
    start = start_ref[...]
    largest = jnp.max(jnp.max(jnp.abs(start), axis=0, keepdims=True), axis=1, keepdims=True)
    exponent = jnp.ceil(jnp.log2(jnp.maximum(largest, 1e-30)))
    sent_ref[:vectors] = start * jnp.exp2(-exponent)
    sent_ref[vectors + 2 * cover :] = jnp.broadcast_to(exponent, (EXTRA, width))
    ones = jnp.ones((16, width), bf16)
    for place, copy in enumerate(large):
        copy.wait()
        if place + AHEAD < len(large):
            large[place + AHEAD].start()
        first = place * LOAD
        terms = [jnp.dot(ones, held_ref[first + i], preferred_element_type=f32)[:8] for i in range(LOAD)]
        for slot, term in enumerate(terms, first):
            if slot < cover:
                total_ref[slot] = term
            else:
                total_ref[cols_ref[0, 0, slot]] += jnp.where(slot < count, term, 0.0)
    for place in range(cover):
        high, low = halves_of(total_ref[place, :1])
        sent_ref[vectors + place : vectors + place + 1] = high
        sent_ref[vectors + cover + place : vectors + cover + place + 1] = low


def load(count, rows, cols, start_block, tiles, cover):
    slots, width = tiles.shape[0], tiles.shape[2]
    vectors = start_block.shape[0]
    places = [pltpu.SMEM(array.shape, jnp.int32) for array in (count, rows, cols)]
    sent = jax.ShapeDtypeStruct((vectors + 2 * cover + EXTRA, width), f32)
    operands = [count, rows, cols] + [pltpu.with_memory_space_constraint(array, pltpu.HBM) for array in (start_block, tiles)]
    return pl.pallas_call(
        load_kernel,
        out_shape=(pltpu.VMEM(tiles.shape, bf16), sent, *places),
        in_specs=[HBM] * 5,
        out_specs=(VMEM, VMEM, SMEM, SMEM, SMEM),
        scratch_shapes=[
            pltpu.VMEM(start_block.shape, f32),
            pltpu.VMEM((cover, 8, width), f32),
            pltpu.SemaphoreType.DMA((slots // LOAD,)),
            pltpu.SemaphoreType.DMA((4,)),
        ],
        compiler_params=pltpu.CompilerParams(vmem_limit_bytes=16 * 2**20),
    )(*operands)


def add_products(transposed, count_ref, take_ref, put_ref, source_ref, held_ref, total_ref):
    count, cover = count_ref[0, 0], total_ref.shape[0]
    contract = (((1,), (1 if transposed else 0,)), ((), ()))

    def product(slot, take):
        return lax.dot_general(source_ref[take], held_ref[slot], contract, preferred_element_type=f32)

    for slot in range(cover):
        total_ref[slot] = product(slot, slot)

    def step(group, carry):
        places, terms = [], []
        for offset in range(GROUP):
            slot = group * GROUP + offset
            term = product(slot, take_ref[0, 0, slot])
            places.append(put_ref[0, 0, slot])
            terms.append(jnp.where(slot < count, term, 0.0))
        for place, term in zip(places, terms):
            total_ref[place] += term
        return carry

    lax.fori_loop(cover // GROUP, (count + GROUP - 1) // GROUP, step, 0)


def first_kernel(
    down, count_ref, take_ref, put_ref, mine_ref, theirs_ref, held_ref, out_ref, scale_ref,
    source_ref, total_ref,
):
    cover, width = total_ref.shape[0], total_ref.shape[2]
    vectors = out_ref.shape[1] - EXTRA
    position = lax.axis_index("row")
    core = lax.rem(position, 2)
    degrees, top = jnp.zeros((cover, width), f32), None
    for place in range(cover // 2):
        pair = mine_ref[place, vectors:] + theirs_ref[place, vectors:]
        degrees += pair[:cover] + pair[cover : 2 * cover] * (1.0 / FINE)
        larger = jnp.maximum(mine_ref[place, vectors + 2 * cover :], theirs_ref[place, vectors + 2 * cover :])
        top = larger if top is None else jnp.maximum(top, larger)
    scales = lax.rsqrt(degrees)
    scales = scales * (1.5 - 0.5 * degrees * scales * scales)
    index = lax.broadcasted_iota(jnp.int32, scales.shape, 0)
    scale_ref[...] = jnp.sum(jnp.where(index == position, scales, 0.0), axis=0, keepdims=True)
    for place in range(cover // 2):
        for other, ref in ((0, mine_ref), (1, theirs_ref)):
            odd = jnp.where(core == 1, 1 - other, other)
            scale = jnp.where(odd == 1, scales[2 * place + 1 : 2 * place + 2], scales[2 * place : 2 * place + 1])
            factor = scale * jnp.exp2(ref[place, vectors + 2 * cover :] - top)[:1]
            source_ref[2 * place + odd, :vectors] = (ref[place, :vectors] * factor).astype(bf16)
            source_ref[2 * place + odd, vectors:] = jnp.ones((16, width), bf16)
    add_products(True, count_ref, take_ref, put_ref, source_ref, held_ref, total_ref)
    out_ref[:, :vectors] = total_ref[:, :vectors] * down
    row = lax.broadcasted_iota(jnp.int32, (EXTRA, width), 0)
    for place in range(cover):
        high, low = halves_of(total_ref[place, vectors : vectors + EXTRA])
        out_ref[place, vectors:] = jnp.where(
            row == 0, high, jnp.where(row == 1, low, jnp.where(row == 2, top, 0.0))
        )


def first_product(count, take, put, mine, theirs, held, vectors, down):
    cover, width = mine.shape[0] * 2, mine.shape[2]
    return pl.pallas_call(
        functools.partial(first_kernel, down),
        out_shape=(
            jax.ShapeDtypeStruct((cover, vectors + EXTRA, width), f32),
            jax.ShapeDtypeStruct((1, width), f32),
        ),
        in_specs=[SMEM, SMEM, SMEM, VMEM, VMEM, VMEM],
        out_specs=(VMEM, VMEM),
        scratch_shapes=[
            pltpu.VMEM((cover, vectors + 16, width), bf16),
            pltpu.VMEM((cover, vectors + 16, width), f32),
        ],
        compiler_params=pltpu.CompilerParams(vmem_limit_bytes=16 * 2**20),
    )(count, take, put, mine, theirs, held)


def forward_kernel(
    down, count_ref, take_ref, put_ref, mine_ref, theirs_ref, held_ref, out_ref,
    source_ref, total_ref,
):
    core = lax.rem(lax.axis_index("row"), 2)
    for place in range(total_ref.shape[0] // 2):
        source_ref[2 * place + core] = mine_ref[place]
        source_ref[2 * place + 1 - core] = theirs_ref[place]
    add_products(True, count_ref, take_ref, put_ref, source_ref, held_ref, total_ref)
    out_ref[...] = total_ref[...] * down


def forward(count, take, put, mine, theirs, held, down):
    total = (mine.shape[0] * 2, *mine.shape[1:])
    return pl.pallas_call(
        functools.partial(forward_kernel, down),
        out_shape=jax.ShapeDtypeStruct(total, f32),
        in_specs=[SMEM, SMEM, SMEM, VMEM, VMEM, VMEM],
        out_specs=VMEM,
        scratch_shapes=[pltpu.VMEM(total, bf16), pltpu.VMEM(total, f32)],
        compiler_params=pltpu.CompilerParams(vmem_limit_bytes=16 * 2**20),
    )(count, take, put, mine, theirs, held)


def backward_kernel(
    down, count_ref, take_ref, put_ref, source_ref, held_ref, keep_ref, give_ref,
    total_ref,
):
    core = lax.rem(lax.axis_index("row"), 2)
    add_products(False, count_ref, take_ref, put_ref, source_ref, held_ref, total_ref)
    for place in range(total_ref.shape[0] // 2):
        keep_ref[place] = total_ref[2 * place + core] * down
        give_ref[place] = total_ref[2 * place + 1 - core] * down


def backward(count, take, put, source, held, down):
    half = jax.ShapeDtypeStruct((source.shape[0] // 2, *source.shape[1:]), f32)
    return pl.pallas_call(
        functools.partial(backward_kernel, down),
        out_shape=(half, half),
        in_specs=[SMEM, SMEM, SMEM, VMEM, VMEM],
        out_specs=(VMEM, VMEM),
        scratch_shapes=[pltpu.VMEM(source.shape, f32)],
        compiler_params=pltpu.CompilerParams(vmem_limit_bytes=16 * 2**20),
    )(count, take, put, source, held)


def on_device(start_block, tile_values, rows, cols, count):
    vectors, piece = start_block.shape
    tiles = tile_values[0, 0]
    slots, width = tiles.shape[0], tiles.shape[2]
    row_parts, col_parts = lax.axis_size("col"), lax.axis_size("row")
    chips = col_parts // 2
    same_core = [[2 * chip + core for chip in range(chips)] for core in range(2)]
    swap = [(index, index ^ 1) for index in range(col_parts)]

    nodes = piece * row_parts * col_parts
    longest = 2 * (slots - col_parts + 1) * width
    down = 2.0 ** math.floor(math.log2(60000.0 / (3.5 * math.sqrt(nodes * longest))))

    def over_chips(parts):
        return lax.all_to_all(parts, "row", 0, 0, axis_index_groups=same_core)

    def over_col(parts):
        return lax.all_to_all(parts, "col", 0, 0)

    def copies(block, parts):
        return jnp.broadcast_to(block[None], (parts, *block.shape))

    def other_core(block):
        return lax.ppermute(block, "row", swap)

    def add_parts(parts):
        return jnp.sum(parts.astype(f32), axis=0) * (1.0 / down)

    held, sent, count, rows, cols = load(count, rows, cols, start_block, tiles, col_parts)
    mine = over_chips(copies(sent.astype(f16), chips))
    theirs = other_core(mine)

    partial, col_scale = first_product(count, cols, rows, mine.astype(f32), theirs.astype(f32), held, vectors, down)
    parts = over_col(partial.astype(f16))
    rest = parts[:, vectors:].astype(f32)
    row_inverse = 1.0 / jnp.sum(rest[:, 0] + rest[:, 1] * (1.0 / FINE), axis=0)
    exponent = jnp.max(rest[:, 2], axis=0)
    factors = jnp.exp2(rest[:, 2] - exponent)
    mixed = add_parts(parts[:, :vectors].astype(f32) * factors[:, None])

    previous = current = None
    for index in range(DEGREE):
        if index:
            mine = over_chips(copies((col_scale * current).astype(bf16), chips))
            partial = forward(count, cols, rows, mine, other_core(mine), held, down)
            mixed = add_parts(over_col(partial.astype(f16)))
        weighted = (mixed * row_inverse).astype(bf16)
        keep, give = backward(count, rows, cols, over_col(copies(weighted, row_parts)), held, down)
        parts = over_chips((keep + other_core(give)).astype(f16))
        if index:
            parts, current, previous, exponent = lax.optimization_barrier((parts, current, previous, exponent))
        else:
            parts, sent, exponent, col_scale = lax.optimization_barrier((parts, sent, exponent, col_scale))
            current = sent[:vectors] * jnp.exp2(sent[vectors + 2 * col_parts] - exponent)
        following = (col_scale * add_parts(parts) - filter_center * current) / filter_half
        if index:
            following = 2.0 * following - previous
        previous, current = current, following
    up = jnp.exp2(exponent)
    return current * up, previous * up


def solution(mesh):
    return jax.shard_map(
        on_device,
        mesh=mesh,
        in_specs=(
            P(None, ("col", "row")),
            P("row", "col", None, None, None),
            P("row", "col", None),
            P("row", "col", None),
            P("row", "col"),
        ),
        out_specs=(P(None, ("col", "row")), P(None, ("col", "row"))),
        check_vma=False,
    )
```

```python
import functools
import math

import jax
import jax.numpy as jnp
from jax import lax
from jax.experimental import pallas as pl
from jax.experimental.pallas import tpu as pltpu
from jax.sharding import PartitionSpec as P

DEGREE = 3
GROUP = 32
LOAD = 8
AHEAD = 6
EXTRA = 8
FINE = 512.0

filter_center = 0.4
filter_half = 0.4

f16, bf16, f32 = jnp.float16, jnp.bfloat16, jnp.float32
SMEM = pl.BlockSpec(memory_space=pltpu.SMEM)
VMEM = pl.BlockSpec(memory_space=pltpu.VMEM)
HBM = pl.BlockSpec(memory_space=pltpu.HBM)


def halves_of(sums):
    high = sums.astype(bf16).astype(f32)
    return high, (sums - high) * FINE


def load_kernel(
    count_in, rows_in, cols_in, start_in, tiles_ref, held_ref, sent_ref, count_ref, rows_ref, cols_ref,
    start_ref, total_ref, done, read,
):
    slots, width = tiles_ref.shape[0], tiles_ref.shape[2]
    vectors, cover = start_ref.shape[0], total_ref.shape[0]
    pairs = ((start_in, start_ref), (count_in, count_ref), (cols_in, cols_ref), (rows_in, rows_ref))
    small = [pltpu.make_async_copy(*pair, read.at[place]) for place, pair in enumerate(pairs)]
    large = [
        pltpu.make_async_copy(tiles_ref.at[pl.ds(first, LOAD)], held_ref.at[pl.ds(first, LOAD)], done.at[place])
        for place, first in enumerate(range(0, slots, LOAD))
    ]
    for copy in small + large[:AHEAD]:
        copy.start()
    for copy in small:
        copy.wait()
    count = count_ref[0, 0]
    start = start_ref[...]
    largest = jnp.max(jnp.max(jnp.abs(start), axis=0, keepdims=True), axis=1, keepdims=True)
    exponent = jnp.ceil(jnp.log2(jnp.maximum(largest, 1e-30)))
    sent_ref[:vectors] = start * jnp.exp2(-exponent)
    sent_ref[vectors + 2 * cover :] = jnp.broadcast_to(exponent, (EXTRA, width))
    ones = jnp.ones((16, width), bf16)
    for place, copy in enumerate(large):
        copy.wait()
        if place + AHEAD < len(large):
            large[place + AHEAD].start()
        first = place * LOAD
        terms = [jnp.dot(ones, held_ref[first + i], preferred_element_type=f32)[:8] for i in range(LOAD)]
        for slot, term in enumerate(terms, first):
            if slot < cover:
                total_ref[slot] = term
            else:
                total_ref[cols_ref[0, 0, slot]] += jnp.where(slot < count, term, 0.0)
    for place in range(cover):
        high, low = halves_of(total_ref[place, :1])
        sent_ref[vectors + place : vectors + place + 1] = high
        sent_ref[vectors + cover + place : vectors + cover + place + 1] = low


def load(count, rows, cols, start_block, tiles, cover):
    slots, width = tiles.shape[0], tiles.shape[2]
    vectors = start_block.shape[0]
    places = [pltpu.SMEM(array.shape, jnp.int32) for array in (count, rows, cols)]
    sent = jax.ShapeDtypeStruct((vectors + 2 * cover + EXTRA, width), f32)
    operands = [count] + [pltpu.with_memory_space_constraint(array, pltpu.HBM) for array in (rows, cols, start_block, tiles)]
    return pl.pallas_call(
        load_kernel,
        out_shape=(pltpu.VMEM(tiles.shape, bf16), sent, *places),
        in_specs=[HBM] * 5,
        out_specs=(VMEM, VMEM, SMEM, SMEM, SMEM),
        scratch_shapes=[
            pltpu.VMEM(start_block.shape, f32),
            pltpu.VMEM((cover, 8, width), f32),
            pltpu.SemaphoreType.DMA((slots // LOAD,)),
            pltpu.SemaphoreType.DMA((4,)),
        ],
        compiler_params=pltpu.CompilerParams(vmem_limit_bytes=16 * 2**20),
    )(*operands)


def add_products(count_ref, take_ref, put_ref, source_ref, held_ref, total_ref, turned_ref=None):
    count, cover = count_ref[0, 0], total_ref.shape[0]

    def product(slot, take):
        tile = held_ref[slot]
        if turned_ref is not None:
            tile = tile.T
            turned_ref[slot] = tile
        return jnp.dot(source_ref[take], tile, preferred_element_type=f32)

    for slot in range(cover):
        total_ref[slot] = product(slot, slot)

    def step(group, carry):
        places, terms = [], []
        for offset in range(GROUP):
            slot = cover + group * GROUP + offset
            term = product(slot, take_ref[0, 0, slot])
            places.append(put_ref[0, 0, slot])
            terms.append(jnp.where(slot < count, term, 0.0))
        for place, term in zip(places, terms):
            total_ref[place] += term
        return carry

    lax.fori_loop(0, (count - cover + GROUP - 1) // GROUP, step, 0)


def first_kernel(
    down, count_ref, take_ref, put_ref, mine_ref, theirs_ref, held_ref, out_ref, scale_ref, turned_ref,
    source_ref, total_ref,
):
    cover, width = total_ref.shape[0], total_ref.shape[2]
    half = width // 2
    vectors = (out_ref.shape[1] - EXTRA) // 2
    position = lax.axis_index("row")
    core = lax.rem(position, 2)
    degrees, top = jnp.zeros((cover, width), f32), None
    for place in range(cover // 2):
        pair = mine_ref[place, vectors:] + theirs_ref[place, vectors:]
        degrees += pair[:cover] + pair[cover : 2 * cover] * (1.0 / FINE)
        larger = jnp.maximum(mine_ref[place, vectors + 2 * cover :], theirs_ref[place, vectors + 2 * cover :])
        top = larger if top is None else jnp.maximum(top, larger)
    scales = lax.rsqrt(degrees)
    scales = scales * (1.5 - 0.5 * degrees * scales * scales)
    index = lax.broadcasted_iota(jnp.int32, scales.shape, 0)
    scale_ref[...] = jnp.sum(jnp.where(index == position, scales, 0.0), axis=0, keepdims=True)
    for place in range(cover // 2):
        for other, ref in ((0, mine_ref), (1, theirs_ref)):
            odd = jnp.where(core == 1, 1 - other, other)
            scale = jnp.where(odd == 1, scales[2 * place + 1 : 2 * place + 2], scales[2 * place : 2 * place + 1])
            factor = scale * jnp.exp2(ref[place, vectors + 2 * cover :] - top)[:1]
            source_ref[2 * place + odd, :vectors] = (ref[place, :vectors] * factor).astype(bf16)
            source_ref[2 * place + odd, vectors:] = jnp.ones((16, width), bf16)
    add_products(count_ref, take_ref, put_ref, source_ref, held_ref, total_ref, turned_ref)
    row = lax.broadcasted_iota(jnp.int32, (EXTRA, half), 0)
    for part in range(2):
        lanes = pl.ds(part * half, half)
        out_ref[:, part * vectors : (part + 1) * vectors] = total_ref[:, :vectors, lanes] * down
    for place in range(cover):
        rest = top[:, :half]
        for part in range(2):
            high, low = halves_of(total_ref[place, vectors : vectors + EXTRA, part * half : (part + 1) * half])
            rest = jnp.where(row == part, high, jnp.where(row == 2 + part, low, rest))
        out_ref[place, 2 * vectors :] = rest


def first_product(count, take, put, mine, theirs, held, vectors, down):
    cover, width = mine.shape[0] * 2, mine.shape[2]
    return pl.pallas_call(
        functools.partial(first_kernel, down),
        out_shape=(
            jax.ShapeDtypeStruct((cover, 2 * vectors + EXTRA, width // 2), f32),
            jax.ShapeDtypeStruct((1, width), f32),
            pltpu.VMEM(held.shape, bf16),
        ),
        in_specs=[SMEM, SMEM, SMEM, VMEM, VMEM, VMEM],
        out_specs=(VMEM, VMEM, VMEM),
        scratch_shapes=[
            pltpu.VMEM((cover, vectors + 16, width), bf16),
            pltpu.VMEM((cover, vectors + 16, width), f32),
        ],
        compiler_params=pltpu.CompilerParams(vmem_limit_bytes=16 * 2**20),
    )(count, take, put, mine, theirs, held)


def forward_kernel(
    down, count_ref, take_ref, put_ref, mine_ref, theirs_ref, held_ref, out_ref,
    source_ref, total_ref,
):
    core = lax.rem(lax.axis_index("row"), 2)
    for place in range(total_ref.shape[0] // 2):
        source_ref[2 * place + core] = mine_ref[place]
        source_ref[2 * place + 1 - core] = theirs_ref[place]
    add_products(count_ref, take_ref, put_ref, source_ref, held_ref, total_ref)
    out_ref[...] = total_ref[...] * down


def forward(count, take, put, mine, theirs, held, down):
    total = (mine.shape[0] * 2, *mine.shape[1:])
    return pl.pallas_call(
        functools.partial(forward_kernel, down),
        out_shape=jax.ShapeDtypeStruct(total, f32),
        in_specs=[SMEM, SMEM, SMEM, VMEM, VMEM, VMEM],
        out_specs=VMEM,
        scratch_shapes=[pltpu.VMEM(total, bf16), pltpu.VMEM(total, f32)],
        compiler_params=pltpu.CompilerParams(vmem_limit_bytes=16 * 2**20),
    )(count, take, put, mine, theirs, held)


def backward_kernel(
    down, count_ref, take_ref, put_ref, source_ref, held_ref, keep_ref, give_ref,
    total_ref,
):
    core = lax.rem(lax.axis_index("row"), 2)
    add_products(count_ref, take_ref, put_ref, source_ref, held_ref, total_ref)
    for place in range(total_ref.shape[0] // 2):
        keep_ref[place] = total_ref[2 * place + core] * down
        give_ref[place] = total_ref[2 * place + 1 - core] * down


def backward(count, take, put, source, held, down):
    half = jax.ShapeDtypeStruct((source.shape[0] // 2, *source.shape[1:]), f32)
    return pl.pallas_call(
        functools.partial(backward_kernel, down),
        out_shape=(half, half),
        in_specs=[SMEM, SMEM, SMEM, VMEM, VMEM],
        out_specs=(VMEM, VMEM),
        scratch_shapes=[pltpu.VMEM(source.shape, f32)],
        compiler_params=pltpu.CompilerParams(vmem_limit_bytes=16 * 2**20),
    )(count, take, put, source, held)


def on_device(start_block, tile_values, rows, cols, count):
    vectors, piece = start_block.shape
    tiles = tile_values[0, 0]
    slots, width = tiles.shape[0], tiles.shape[2]
    row_parts, col_parts = lax.axis_size("col"), lax.axis_size("row")
    chips = col_parts // 2
    same_core = [[2 * chip + core for chip in range(chips)] for core in range(2)]
    swap = [(index, index ^ 1) for index in range(col_parts)]

    nodes = piece * row_parts * col_parts
    longest = 2 * (slots - col_parts + 1) * width
    down = 2.0 ** math.floor(math.log2(60000.0 / (3.5 * math.sqrt(nodes * longest))))

    def over_chips(parts):
        return lax.all_to_all(parts, "row", 0, 0, axis_index_groups=same_core)

    def over_col(parts):
        return lax.all_to_all(parts, "col", 0, 0)

    def copies(block, parts):
        return jnp.broadcast_to(block[None], (parts, *block.shape))

    def other_core(block):
        return lax.ppermute(block, "row", swap)

    def add_parts(parts):
        return jnp.sum(parts.astype(f32), axis=0) * (1.0 / down)

    held, sent, count, rows, cols = load(count, rows, cols, start_block, tiles, col_parts)
    mine = over_chips(copies(sent.astype(f16), chips))
    theirs = other_core(mine)

    partial, col_scale, turned = first_product(
        count, cols, rows, mine.astype(f32), theirs.astype(f32), held, vectors, down
    )
    parts = over_col(partial.astype(f16)).astype(f32)
    rest = parts[:, 2 * vectors :]
    wide = [jnp.concatenate([rest[:, 2 * i], rest[:, 2 * i + 1]], axis=1) for i in range(3)]
    row_inverse = 1.0 / jnp.sum(wide[0] + wide[1] * (1.0 / FINE), axis=0)
    exponent = jnp.max(wide[2], axis=0)
    factors = jnp.exp2(wide[2] - exponent)[:, None]
    whole = jnp.concatenate([parts[:, :vectors], parts[:, vectors : 2 * vectors]], axis=2)
    mixed = add_parts(whole * factors)

    previous = current = None
    for index in range(DEGREE):
        if index:
            mine = over_chips(copies((col_scale * current).astype(bf16), chips))
            partial = forward(count, cols, rows, mine, other_core(mine), turned, down)
            mixed = add_parts(over_col(partial.astype(f16)))
        weighted = (mixed * row_inverse).astype(bf16)
        keep, give = backward(count, rows, cols, over_col(copies(weighted, row_parts)), held, down)
        parts = over_chips((keep + other_core(give.astype(f16)).astype(f32)).astype(f16))
        if index:
            parts, current, previous, exponent = lax.optimization_barrier((parts, current, previous, exponent))
        else:
            parts, sent, exponent, col_scale = lax.optimization_barrier((parts, sent, exponent, col_scale))
            current = sent[:vectors] * jnp.exp2(sent[vectors + 2 * col_parts] - exponent)
        following = (col_scale * add_parts(parts) - filter_center * current) / filter_half
        if index:
            following = 2.0 * following - previous
        previous, current = current, following
    up = jnp.exp2(exponent)
    return current * up, previous * up


def solution(mesh):
    return jax.shard_map(
        on_device,
        mesh=mesh,
        in_specs=(
            P(None, ("col", "row")),
            P("row", "col", None, None, None),
            P("row", "col", None),
            P("row", "col", None),
            P("row", "col"),
        ),
        out_specs=(P(None, ("col", "row")), P(None, ("col", "row"))),
        check_vma=False,
    )
```

```python
import functools
import math

import jax
import jax.numpy as jnp
from jax import lax
from jax.experimental import pallas as pl
from jax.experimental.pallas import tpu as pltpu
from jax.sharding import PartitionSpec as P

DEGREE = 3
GROUP = 32
SMALL = 8
LOAD = 8
AHEAD = 6
EXTRA = 8
FINE = 512.0

filter_center = 0.4
filter_half = 0.4

f16, bf16, f32 = jnp.float16, jnp.bfloat16, jnp.float32
SMEM = pl.BlockSpec(memory_space=pltpu.SMEM)
VMEM = pl.BlockSpec(memory_space=pltpu.VMEM)
HBM = pl.BlockSpec(memory_space=pltpu.HBM)


def halves_of(sums):
    high = sums.astype(bf16).astype(f32)
    return high, (sums - high) * FINE


def load_kernel(
    count_in, rows_in, cols_in, start_in, tiles_ref, held_ref, sent_ref, count_ref, rows_ref, cols_ref,
    start_ref, total_ref, done, read,
):
    slots, width = tiles_ref.shape[0], tiles_ref.shape[2]
    vectors, cover = start_ref.shape[0], total_ref.shape[0]
    pairs = ((start_in, start_ref), (count_in, count_ref), (cols_in, cols_ref), (rows_in, rows_ref))
    small = [pltpu.make_async_copy(*pair, read.at[place]) for place, pair in enumerate(pairs)]
    large = [
        pltpu.make_async_copy(tiles_ref.at[pl.ds(first, LOAD)], held_ref.at[pl.ds(first, LOAD)], done.at[place])
        for place, first in enumerate(range(0, slots, LOAD))
    ]
    for copy in small + large[: cover // LOAD]:
        copy.start()
    for copy in small:
        copy.wait()
    count = count_ref[0, 0]

    def if_live(place, work):
        pl.when(place * LOAD < count)(work)

    for place in range(cover // LOAD, AHEAD):
        if_live(place, large[place].start)
    start = start_ref[...]
    largest = jnp.max(jnp.max(jnp.abs(start), axis=0, keepdims=True), axis=1, keepdims=True)
    exponent = jnp.ceil(jnp.log2(jnp.maximum(largest, 1e-30)))
    sent_ref[:vectors] = start * jnp.exp2(-exponent)
    sent_ref[vectors + cover :] = jnp.broadcast_to(exponent, (EXTRA, width))
    ones = jnp.ones((16, width), bf16)

    def add(place):
        large[place].wait()
        if place + AHEAD < len(large):
            if_live(place + AHEAD, large[place + AHEAD].start)
        first = place * LOAD
        terms = [jnp.dot(ones, held_ref[first + i], preferred_element_type=f32)[:8] for i in range(LOAD)]
        for slot, term in enumerate(terms, first):
            if slot < cover:
                total_ref[slot] = term
            else:
                total_ref[cols_ref[0, 0, slot]] += jnp.where(slot < count, term, 0.0)

    for place in range(len(large)):
        if place * LOAD < cover:
            add(place)
        else:
            if_live(place, functools.partial(add, place))
    for place in range(cover):
        sent_ref[vectors + place : vectors + place + 1] = total_ref[place, :1]


def load(count, rows, cols, start_block, tiles, cover):
    slots, width = tiles.shape[0], tiles.shape[2]
    vectors = start_block.shape[0]
    places = [pltpu.SMEM(array.shape, jnp.int32) for array in (count, rows, cols)]
    sent = jax.ShapeDtypeStruct((vectors + cover + EXTRA, width), f32)
    operands = [count] + [pltpu.with_memory_space_constraint(array, pltpu.HBM) for array in (rows, cols, start_block, tiles)]
    return pl.pallas_call(
        load_kernel,
        out_shape=(pltpu.VMEM(tiles.shape, bf16), sent, *places),
        in_specs=[HBM] * 5,
        out_specs=(VMEM, VMEM, SMEM, SMEM, SMEM),
        scratch_shapes=[
            pltpu.VMEM(start_block.shape, f32),
            pltpu.VMEM((cover, 8, width), f32),
            pltpu.SemaphoreType.DMA((slots // LOAD,)),
            pltpu.SemaphoreType.DMA((4,)),
        ],
        compiler_params=pltpu.CompilerParams(vmem_limit_bytes=16 * 2**20),
    )(*operands)


def add_products(count_ref, take_ref, put_ref, source_ref, held_ref, total_ref, turned_ref=None, order=lambda place: place):
    count, cover = count_ref[0, 0], total_ref.shape[0]

    def product(slot, take):
        tile = held_ref[slot]
        if turned_ref is not None:
            tile = tile.T
            turned_ref[slot] = tile
        return jnp.dot(source_ref[take], tile, preferred_element_type=f32)

    for slot in range(cover):
        total_ref[order(slot)] = product(slot, slot)

    def add(first, group):
        places, terms = [], []
        for offset in range(group):
            slot = first + offset
            term = product(slot, take_ref[0, 0, slot])
            places.append(order(put_ref[0, 0, slot]))
            terms.append(jnp.where(slot < count, term, 0.0))
        for place, term in zip(places, terms):
            total_ref[place] += term

    large = (count - cover + GROUP // 2 - 1) // GROUP
    after = cover + large * GROUP
    lax.fori_loop(0, large, lambda index, _: add(cover + index * GROUP, GROUP), None)
    small = jnp.maximum(count - after + SMALL - 1, 0) // SMALL
    lax.fori_loop(0, small, lambda index, _: add(after + index * SMALL, SMALL), None)


def first_kernel(
    down, count_ref, take_ref, put_ref, mine_ref, theirs_ref, held_ref, out_ref, scale_ref, turned_ref,
    source_ref, total_ref,
):
    cover, width = total_ref.shape[0], total_ref.shape[2]
    half = width // 2
    vectors = (out_ref.shape[1] - EXTRA) // 2
    position = lax.axis_index("row")
    core = lax.rem(position, 2)
    degrees, top = jnp.zeros((cover, width), f32), None
    for place in range(cover // 2):
        degrees += mine_ref[place, vectors : vectors + cover] + theirs_ref[place, vectors : vectors + cover]
        larger = jnp.maximum(mine_ref[place, vectors + cover :], theirs_ref[place, vectors + cover :])
        top = larger if top is None else jnp.maximum(top, larger)
    scales = lax.rsqrt(degrees)
    scales = scales * (1.5 - 0.5 * degrees * scales * scales)
    index = lax.broadcasted_iota(jnp.int32, scales.shape, 0)
    scale_ref[...] = jnp.sum(jnp.where(index == position, scales, 0.0), axis=0, keepdims=True)
    for place in range(cover // 2):
        for other, ref in ((0, mine_ref), (1, theirs_ref)):
            odd = jnp.where(core == 1, 1 - other, other)
            scale = jnp.where(odd == 1, scales[2 * place + 1 : 2 * place + 2], scales[2 * place : 2 * place + 1])
            factor = scale * down * jnp.exp2(ref[place, vectors + cover :] - top)[:1]
            source_ref[2 * place + odd, :vectors] = (ref[place, :vectors] * factor).astype(bf16)
            source_ref[2 * place + odd, vectors:] = jnp.ones((16, width), bf16)
    add_products(count_ref, take_ref, put_ref, source_ref, held_ref, total_ref, turned_ref)
    row = lax.broadcasted_iota(jnp.int32, (EXTRA, half), 0)
    for part in range(2):
        lanes = pl.ds(part * half, half)
        out_ref[:, part * vectors : (part + 1) * vectors] = total_ref[:, :vectors, lanes]
    for place in range(cover):
        rest = top[:, :half]
        for part in range(2):
            high, low = halves_of(total_ref[place, vectors : vectors + EXTRA, part * half : (part + 1) * half])
            rest = jnp.where(row == part, high, jnp.where(row == 2 + part, low, rest))
        out_ref[place, 2 * vectors :] = rest


def first_product(count, take, put, mine, theirs, held, vectors, down):
    cover, width = mine.shape[0] * 2, mine.shape[2]
    return pl.pallas_call(
        functools.partial(first_kernel, down),
        out_shape=(
            jax.ShapeDtypeStruct((cover, 2 * vectors + EXTRA, width // 2), f32),
            jax.ShapeDtypeStruct((1, width), f32),
            pltpu.VMEM(held.shape, bf16),
        ),
        in_specs=[SMEM, SMEM, SMEM, VMEM, VMEM, VMEM],
        out_specs=(VMEM, VMEM, VMEM),
        scratch_shapes=[
            pltpu.VMEM((cover, vectors + 16, width), bf16),
            pltpu.VMEM((cover, vectors + 16, width), f32),
        ],
        compiler_params=pltpu.CompilerParams(vmem_limit_bytes=16 * 2**20),
    )(count, take, put, mine, theirs, held)


def forward_kernel(count_ref, take_ref, put_ref, mine_ref, theirs_ref, held_ref, total_ref, source_ref):
    core = lax.rem(lax.axis_index("row"), 2)
    for place in range(total_ref.shape[0] // 2):
        source_ref[2 * place + core] = mine_ref[place]
        source_ref[2 * place + 1 - core] = theirs_ref[place]
    add_products(count_ref, take_ref, put_ref, source_ref, held_ref, total_ref)


def forward(count, take, put, mine, theirs, held):
    total = (mine.shape[0] * 2, *mine.shape[1:])
    return pl.pallas_call(
        forward_kernel,
        out_shape=jax.ShapeDtypeStruct(total, f32),
        in_specs=[SMEM, SMEM, SMEM, VMEM, VMEM, VMEM],
        out_specs=VMEM,
        scratch_shapes=[pltpu.VMEM(total, bf16)],
        compiler_params=pltpu.CompilerParams(vmem_limit_bytes=16 * 2**20),
    )(count, take, put, mine, theirs, held)


def backward_kernel(count_ref, take_ref, put_ref, source_ref, held_ref, total_ref):
    core, half = lax.rem(lax.axis_index("row"), 2), total_ref.shape[0] // 2

    def order(place):
        return jnp.where(place % 2 == core, 0, half) + place // 2

    add_products(count_ref, take_ref, put_ref, source_ref, held_ref, total_ref, order=order)


def backward(count, take, put, source, held):
    total = pl.pallas_call(
        backward_kernel,
        out_shape=jax.ShapeDtypeStruct(source.shape, f32),
        in_specs=[SMEM, SMEM, SMEM, VMEM, VMEM],
        out_specs=VMEM,
        compiler_params=pltpu.CompilerParams(vmem_limit_bytes=16 * 2**20),
    )(count, take, put, source, held)
    half = source.shape[0] // 2
    return total[:half], total[half:]


def on_device(start_block, tile_values, rows, cols, count):
    vectors, piece = start_block.shape
    tiles = tile_values[0, 0]
    slots, width = tiles.shape[0], tiles.shape[2]
    row_parts, col_parts = lax.axis_size("col"), lax.axis_size("row")
    chips = col_parts // 2
    same_core = [[2 * chip + core for chip in range(chips)] for core in range(2)]
    swap = [(index, index ^ 1) for index in range(col_parts)]

    nodes = piece * row_parts * col_parts
    longest = 2 * (slots - col_parts + 1) * width
    down = 2.0 ** math.floor(math.log2(60000.0 / (3.5 * math.sqrt(nodes * longest))))

    def over_chips(parts):
        return lax.all_to_all(parts, "row", 0, 0, axis_index_groups=same_core)

    def over_col(parts):
        return lax.all_to_all(parts, "col", 0, 0)

    def copies(block, parts):
        return jnp.broadcast_to(block[None], (parts, *block.shape))

    def other_core(block):
        return lax.ppermute(block, "row", swap)

    def add_parts(parts):
        return jnp.sum(parts.astype(f32), axis=0)

    held, sent, count, rows, cols = load(count, rows, cols, start_block, tiles, col_parts)
    mine = over_chips(copies(sent.astype(f16), chips))
    theirs = other_core(mine)

    partial, col_scale, turned = first_product(
        count, cols, rows, mine.astype(f32), theirs.astype(f32), held, vectors, down
    )
    parts = over_col(partial.astype(f16)).astype(f32)
    rest = parts[:, 2 * vectors :]
    wide = [jnp.concatenate([rest[:, 2 * i], rest[:, 2 * i + 1]], axis=1) for i in range(3)]
    row_inverse = 1.0 / jnp.sum(wide[0] + wide[1] * (1.0 / FINE), axis=0)
    exponent = jnp.max(wide[2], axis=0)
    factors = jnp.exp2(wide[2] - exponent)[:, None]
    whole = jnp.concatenate([parts[:, :vectors], parts[:, vectors : 2 * vectors]], axis=2)
    mixed = add_parts(whole * factors)

    previous = current = None
    for index in range(DEGREE):
        if index:
            mine = over_chips(copies((col_scale * down * current).astype(bf16), chips))
            partial = forward(count, cols, rows, mine, other_core(mine), turned)
            mixed = add_parts(over_col(partial.astype(f16)))
        weighted = (mixed * row_inverse).astype(bf16)
        keep, give = backward(count, rows, cols, over_col(copies(weighted, row_parts)), held)
        parts = over_chips((keep + other_core(give.astype(f16)).astype(f32)).astype(f16))
        if index:
            parts, current, previous, exponent = lax.optimization_barrier((parts, current, previous, exponent))
        else:
            parts, sent, exponent, col_scale = lax.optimization_barrier((parts, sent, exponent, col_scale))
            current = sent[:vectors] * jnp.exp2(sent[vectors + col_parts] - exponent)
        following = (col_scale * (1.0 / down) * add_parts(parts) - filter_center * current) / filter_half
        if index:
            following = 2.0 * following - previous
        previous, current = current, following
    up = jnp.exp2(exponent)
    return current * up, previous * up


def solution(mesh):
    return jax.shard_map(
        on_device,
        mesh=mesh,
        in_specs=(
            P(None, ("col", "row")),
            P("row", "col", None, None, None),
            P("row", "col", None),
            P("row", "col", None),
            P("row", "col"),
        ),
        out_specs=(P(None, ("col", "row")), P(None, ("col", "row"))),
        check_vma=False,
    )
```

```python
import functools
import math

import jax
import jax.numpy as jnp
from jax import lax
from jax.experimental import pallas as pl
from jax.experimental.pallas import tpu as pltpu
from jax.sharding import PartitionSpec as P

DEGREE = 3
GROUP = 32
SMALL = 8
LOAD = 8
AHEAD = 6
EXTRA = 8
FINE = 512.0

filter_center = 0.4
filter_half = 0.4

f16, bf16, f32 = jnp.float16, jnp.bfloat16, jnp.float32
SMEM = pl.BlockSpec(memory_space=pltpu.SMEM)
VMEM = pl.BlockSpec(memory_space=pltpu.VMEM)
HBM = pl.BlockSpec(memory_space=pltpu.HBM)


def halves_of(sums):
    high = sums.astype(bf16).astype(f32)
    return high, (sums - high) * FINE


def load_kernel(
    count_in, rows_in, cols_in, start_in, tiles_ref, held_ref, turned_ref, sent_ref, count_ref, rows_ref, cols_ref,
    sorted_ref, start_ref, total_ref, done, read,
):
    slots, width = tiles_ref.shape[0], tiles_ref.shape[2]
    vectors, cover = start_ref.shape[0], total_ref.shape[0]
    pairs = ((start_in, start_ref), (count_in, count_ref), (cols_in, cols_ref), (rows_in, rows_ref))
    small = [pltpu.make_async_copy(*pair, read.at[place]) for place, pair in enumerate(pairs)]
    large = [
        pltpu.make_async_copy(tiles_ref.at[pl.ds(first, LOAD)], held_ref.at[pl.ds(first, LOAD)], done.at[place])
        for place, first in enumerate(range(0, slots, LOAD))
    ]
    for copy in small + large[: cover // LOAD]:
        copy.start()
    for copy in small:
        copy.wait()
    count = count_ref[0, 0]

    def if_live(place, work):
        pl.when(place * LOAD < count)(work)

    for place in range(cover // LOAD, AHEAD):
        if_live(place, large[place].start)
    core = lax.rem(lax.axis_index("row"), 2)

    def sort(slot, numbers):
        side = jnp.where(cols_ref[0, 0, slot] % 2 == core, 0, 1)
        sorted_ref[side, jnp.where(side == 0, *numbers)] = slot
        return numbers[0] + 1 - side, numbers[1] + side

    numbers = lax.fori_loop(cover, count, sort, (0, 0))
    for side in range(2):
        sorted_ref[side, slots - cover] = numbers[side]
    start = start_ref[...]
    largest = jnp.max(jnp.max(jnp.abs(start), axis=0, keepdims=True), axis=1, keepdims=True)
    exponent = jnp.ceil(jnp.log2(jnp.maximum(largest, 1e-30)))
    sent_ref[:vectors] = start * jnp.exp2(-exponent)
    sent_ref[vectors + cover :] = jnp.broadcast_to(exponent, (EXTRA, width))
    ones = jnp.ones((16, width), bf16)

    def add(place):
        large[place].wait()
        if place + AHEAD < len(large):
            if_live(place + AHEAD, large[place + AHEAD].start)
        first = place * LOAD
        terms = [jnp.dot(ones, held_ref[first + i], preferred_element_type=f32)[:8] for i in range(LOAD)]
        for slot, term in enumerate(terms, first):
            turned_ref[slot] = held_ref[slot].T
            if slot < cover:
                total_ref[slot] = term
            else:
                total_ref[cols_ref[0, 0, slot]] += jnp.where(slot < count, term, 0.0)

    for place in range(len(large)):
        if place * LOAD < cover:
            add(place)
        else:
            if_live(place, functools.partial(add, place))
    for place in range(cover):
        sent_ref[vectors + place : vectors + place + 1] = total_ref[place, :1]


def load(count, rows, cols, start_block, tiles, cover):
    slots, width = tiles.shape[0], tiles.shape[2]
    vectors = start_block.shape[0]
    places = [pltpu.SMEM(array.shape, jnp.int32) for array in (count, rows, cols)]
    places.append(pltpu.SMEM((2, slots - cover + 1), jnp.int32))
    sent = jax.ShapeDtypeStruct((vectors + cover + EXTRA, width), f32)
    operands = [count] + [pltpu.with_memory_space_constraint(array, pltpu.HBM) for array in (rows, cols, start_block, tiles)]
    return pl.pallas_call(
        load_kernel,
        out_shape=(pltpu.VMEM(tiles.shape, bf16), pltpu.VMEM(tiles.shape, bf16), sent, *places),
        in_specs=[HBM] * 5,
        out_specs=(VMEM, VMEM, VMEM, SMEM, SMEM, SMEM, SMEM),
        scratch_shapes=[
            pltpu.VMEM(start_block.shape, f32),
            pltpu.VMEM((cover, 8, width), f32),
            pltpu.SemaphoreType.DMA((slots // LOAD,)),
            pltpu.SemaphoreType.DMA((4,)),
        ],
        compiler_params=pltpu.CompilerParams(vmem_limit_bytes=16 * 2**20),
    )(*operands)


def add_products(count_ref, take_ref, put_ref, source_ref, held_ref, total_ref):
    count, cover = count_ref[0, 0], total_ref.shape[0]

    def product(slot, take):
        return jnp.dot(source_ref[take], held_ref[slot], preferred_element_type=f32)

    for slot in range(cover):
        total_ref[slot] = product(slot, slot)

    def add(first, group):
        places, terms = [], []
        for offset in range(group):
            slot = first + offset
            term = product(slot, take_ref[0, 0, slot])
            places.append(put_ref[0, 0, slot])
            terms.append(jnp.where(slot < count, term, 0.0))
        for place, term in zip(places, terms):
            total_ref[place] += term

    in_steps(cover, count, add)


def in_steps(first, end, add):
    large = (end - first + GROUP // 2 - 1) // GROUP
    after = first + large * GROUP
    lax.fori_loop(0, large, lambda index, _: add(first + index * GROUP, GROUP), None)
    small = jnp.maximum(end - after + SMALL - 1, 0) // SMALL
    lax.fori_loop(0, small, lambda index, _: add(after + index * SMALL, SMALL), None)


def add_side(side, sorted_ref, take_ref, put_ref, held_ref, source, total_ref, place, first):
    core, cover = lax.rem(lax.axis_index("row"), 2), take_ref.shape[2] + 1 - sorted_ref.shape[1]
    number = sorted_ref[side, sorted_ref.shape[1] - 1]

    def product(slot, take):
        return jnp.dot(source(take), held_ref[slot], preferred_element_type=f32)

    for index in range(cover // 2):
        slot = 2 * index + (core if side == 0 else 1 - core)
        term = product(slot, slot)
        if first:
            total_ref[place(slot)] = term
        else:
            total_ref[place(slot)] += term

    def add(start, group):
        places, terms = [], []
        for offset in range(group):
            index = start + offset
            slot = jnp.where(index < number, sorted_ref[side, index], 0)
            places.append(place(put_ref[0, 0, slot]))
            terms.append(jnp.where(index < number, product(slot, take_ref[0, 0, slot]), 0.0))
        for into, term in zip(places, terms):
            total_ref[into] += term

    in_steps(0, number, add)


def first_kernel(
    down, count_ref, take_ref, put_ref, mine_ref, theirs_ref, held_ref, out_ref, scale_ref,
    source_ref, total_ref,
):
    cover, width = total_ref.shape[0], total_ref.shape[2]
    half = width // 2
    vectors = (out_ref.shape[1] - EXTRA) // 2
    position = lax.axis_index("row")
    core = lax.rem(position, 2)
    degrees, top = jnp.zeros((cover, width), f32), None
    for place in range(cover // 2):
        degrees += mine_ref[place, vectors : vectors + cover] + theirs_ref[place, vectors : vectors + cover]
        larger = jnp.maximum(mine_ref[place, vectors + cover :], theirs_ref[place, vectors + cover :])
        top = larger if top is None else jnp.maximum(top, larger)
    scales = lax.rsqrt(degrees)
    scales = scales * (1.5 - 0.5 * degrees * scales * scales)
    index = lax.broadcasted_iota(jnp.int32, scales.shape, 0)
    scale_ref[...] = jnp.sum(jnp.where(index == position, scales, 0.0), axis=0, keepdims=True)
    for place in range(cover // 2):
        for other, ref in ((0, mine_ref), (1, theirs_ref)):
            odd = jnp.where(core == 1, 1 - other, other)
            scale = jnp.where(odd == 1, scales[2 * place + 1 : 2 * place + 2], scales[2 * place : 2 * place + 1])
            factor = scale * down * jnp.exp2(ref[place, vectors + cover :] - top)[:1]
            source_ref[2 * place + odd, :vectors] = (ref[place, :vectors] * factor).astype(bf16)
            source_ref[2 * place + odd, vectors:] = jnp.ones((16, width), bf16)
    add_products(count_ref, take_ref, put_ref, source_ref, held_ref, total_ref)
    row = lax.broadcasted_iota(jnp.int32, (EXTRA, half), 0)
    for part in range(2):
        lanes = pl.ds(part * half, half)
        out_ref[:, part * vectors : (part + 1) * vectors] = total_ref[:, :vectors, lanes]
    for place in range(cover):
        rest = top[:, :half]
        for part in range(2):
            high, low = halves_of(total_ref[place, vectors : vectors + EXTRA, part * half : (part + 1) * half])
            rest = jnp.where(row == part, high, jnp.where(row == 2 + part, low, rest))
        out_ref[place, 2 * vectors :] = rest


def first_product(count, take, put, mine, theirs, held, vectors, down):
    cover, width = mine.shape[0] * 2, mine.shape[2]
    return pl.pallas_call(
        functools.partial(first_kernel, down),
        out_shape=(
            jax.ShapeDtypeStruct((cover, 2 * vectors + EXTRA, width // 2), f32),
            jax.ShapeDtypeStruct((1, width), f32),
        ),
        in_specs=[SMEM, SMEM, SMEM, VMEM, VMEM, VMEM],
        out_specs=(VMEM, VMEM),
        scratch_shapes=[
            pltpu.VMEM((cover, vectors + 16, width), bf16),
            pltpu.VMEM((cover, vectors + 16, width), f32),
        ],
        compiler_params=pltpu.CompilerParams(vmem_limit_bytes=16 * 2**20),
    )(count, take, put, mine, theirs, held)


def forward_kernel(side, sorted_ref, take_ref, put_ref, source_ref, held_ref, *refs):
    total_ref, core = refs[-1], lax.rem(lax.axis_index("row"), 2)
    if side == 0:
        for index in range(total_ref.shape[0] // 2):
            total_ref[2 * index + 1 - core] = jnp.zeros(total_ref.shape[1:], f32)
    add_side(
        side, sorted_ref, take_ref, put_ref, held_ref, lambda take: source_ref[take // 2], total_ref, lambda p: p, side == 0
    )


def forward(side, places, take, put, source, held, total=None):
    shape = (source.shape[0] * 2, *source.shape[1:])
    return pl.pallas_call(
        functools.partial(forward_kernel, side),
        out_shape=jax.ShapeDtypeStruct(shape, f32),
        in_specs=[SMEM, SMEM, SMEM, VMEM, VMEM] + [VMEM] * side,
        out_specs=VMEM,
        input_output_aliases={5: 0} if side else {},
        compiler_params=pltpu.CompilerParams(vmem_limit_bytes=16 * 2**20),
    )(places, take, put, source, held, *([total] if side else []))


def backward_kernel(side, sorted_ref, take_ref, put_ref, source_ref, held_ref, total_ref):
    add_side(
        side, sorted_ref, take_ref, put_ref, held_ref, lambda take: source_ref[take], total_ref, lambda p: p // 2, True
    )


def backward(side, places, take, put, source, held):
    return pl.pallas_call(
        functools.partial(backward_kernel, side),
        out_shape=jax.ShapeDtypeStruct((source.shape[0] // 2, *source.shape[1:]), f32),
        in_specs=[SMEM, SMEM, SMEM, VMEM, VMEM],
        out_specs=VMEM,
        compiler_params=pltpu.CompilerParams(vmem_limit_bytes=16 * 2**20),
    )(places, take, put, source, held)


def on_device(start_block, tile_values, rows, cols, count):
    vectors, piece = start_block.shape
    tiles = tile_values[0, 0]
    slots, width = tiles.shape[0], tiles.shape[2]
    row_parts, col_parts = lax.axis_size("col"), lax.axis_size("row")
    chips = col_parts // 2
    same_core = [[2 * chip + core for chip in range(chips)] for core in range(2)]
    swap = [(index, index ^ 1) for index in range(col_parts)]

    nodes = piece * row_parts * col_parts
    longest = 2 * (slots - col_parts + 1) * width
    down = 2.0 ** math.floor(math.log2(60000.0 / (3.5 * math.sqrt(nodes * longest))))

    def over_chips(parts):
        return lax.all_to_all(parts, "row", 0, 0, axis_index_groups=same_core)

    def over_col(parts):
        return lax.all_to_all(parts, "col", 0, 0)

    def copies(block, parts):
        return jnp.broadcast_to(block[None], (parts, *block.shape))

    def other_core(block):
        return lax.ppermute(block, "row", swap)

    def add_parts(parts):
        return jnp.sum(parts.astype(f32), axis=0)

    held, turned, sent, count, rows, cols, places = load(count, rows, cols, start_block, tiles, col_parts)
    mine = over_chips(copies(sent.astype(f16), chips))
    theirs = other_core(mine)

    partial, col_scale = first_product(
        count, cols, rows, mine.astype(f32), theirs.astype(f32), turned, vectors, down
    )
    parts = over_col(partial.astype(f16)).astype(f32)
    rest = parts[:, 2 * vectors :]
    wide = [jnp.concatenate([rest[:, 2 * i], rest[:, 2 * i + 1]], axis=1) for i in range(3)]
    row_inverse = 1.0 / jnp.sum(wide[0] + wide[1] * (1.0 / FINE), axis=0)
    exponent = jnp.max(wide[2], axis=0)
    factors = jnp.exp2(wide[2] - exponent)[:, None]
    whole = jnp.concatenate([parts[:, :vectors], parts[:, vectors : 2 * vectors]], axis=2)
    mixed = add_parts(whole * factors)

    previous = current = None
    for index in range(DEGREE):
        if index:
            mine = over_chips(copies((col_scale * down * current).astype(bf16), chips))
            theirs = other_core(mine)
            partial = forward(0, places, cols, rows, mine, turned)
            partial = forward(1, places, cols, rows, theirs, turned, partial)
            mixed = add_parts(over_col(partial.astype(f16)))
        weighted = (mixed * row_inverse).astype(bf16)
        gathered = over_col(copies(weighted, row_parts))
        given = other_core(backward(1, places, rows, cols, gathered, held).astype(f16))
        keep = backward(0, places, rows, cols, gathered, held)
        parts = over_chips((keep + given.astype(f32)).astype(f16))
        if index:
            parts, current, previous, exponent = lax.optimization_barrier((parts, current, previous, exponent))
        else:
            parts, sent, exponent, col_scale = lax.optimization_barrier((parts, sent, exponent, col_scale))
            current = sent[:vectors] * jnp.exp2(sent[vectors + col_parts] - exponent)
        following = (col_scale * (1.0 / down) * add_parts(parts) - filter_center * current) / filter_half
        if index:
            following = 2.0 * following - previous
        previous, current = current, following
    up = jnp.exp2(exponent)
    return current * up, previous * up


def solution(mesh):
    return jax.shard_map(
        on_device,
        mesh=mesh,
        in_specs=(
            P(None, ("col", "row")),
            P("row", "col", None, None, None),
            P("row", "col", None),
            P("row", "col", None),
            P("row", "col"),
        ),
        out_specs=(P(None, ("col", "row")), P(None, ("col", "row"))),
        check_vma=False,
    )
```

```python
import functools
import math

import jax
import jax.numpy as jnp
from jax import lax
from jax.experimental import pallas as pl
from jax.experimental.pallas import tpu as pltpu
from jax.sharding import PartitionSpec as P

DEGREE = 3
GROUP = 32
SMALL = 8
LOAD = 8
AHEAD = 6
EXTRA = 8
FINE = 512.0

filter_center = 0.4
filter_half = 0.4

f16, bf16, f32 = jnp.float16, jnp.bfloat16, jnp.float32
SMEM = pl.BlockSpec(memory_space=pltpu.SMEM)
VMEM = pl.BlockSpec(memory_space=pltpu.VMEM)
HBM = pl.BlockSpec(memory_space=pltpu.HBM)


def halves_of(sums):
    high = sums.astype(bf16).astype(f32)
    return high, (sums - high) * FINE


def load_kernel(
    count_in, rows_in, cols_in, start_in, tiles_ref, held_ref, turned_ref, sent_ref, count_ref, rows_ref, cols_ref,
    sorted_ref, start_ref, total_ref, done, read,
):
    slots, width = tiles_ref.shape[0], tiles_ref.shape[2]
    vectors, cover = start_ref.shape[0], total_ref.shape[0]
    pairs = ((start_in, start_ref), (count_in, count_ref), (cols_in, cols_ref), (rows_in, rows_ref))
    small = [pltpu.make_async_copy(*pair, read.at[place]) for place, pair in enumerate(pairs)]
    large = [
        pltpu.make_async_copy(tiles_ref.at[pl.ds(first, LOAD)], held_ref.at[pl.ds(first, LOAD)], done.at[place])
        for place, first in enumerate(range(0, slots, LOAD))
    ]
    for copy in small + large[: cover // LOAD]:
        copy.start()
    for copy in small:
        copy.wait()
    count = count_ref[0, 0]

    def if_live(place, work):
        pl.when(place * LOAD < count)(work)

    for place in range(cover // LOAD, AHEAD):
        if_live(place, large[place].start)
    core = lax.rem(lax.axis_index("row"), 2)

    last = slots - cover
    for side in range(2):
        sorted_ref[side, last] = 0

    def sort(slot):
        side = jnp.where(cols_ref[0, 0, slot] % 2 == core, 0, 1)
        number = sorted_ref[side, last]
        sorted_ref[side, number] = slot
        sorted_ref[side, last] = number + jnp.where(slot < count, 1, 0)

    start = start_ref[...]
    largest = jnp.max(jnp.max(jnp.abs(start), axis=0, keepdims=True), axis=1, keepdims=True)
    exponent = jnp.ceil(jnp.log2(jnp.maximum(largest, 1e-30)))
    sent_ref[:vectors] = start * jnp.exp2(-exponent)
    sent_ref[vectors + cover :] = jnp.broadcast_to(exponent, (EXTRA, width))
    ones = jnp.ones((16, width), bf16)

    def add(place):
        large[place].wait()
        if place + AHEAD < len(large):
            if_live(place + AHEAD, large[place + AHEAD].start)
        first = place * LOAD
        terms = [jnp.dot(ones, held_ref[first + i], preferred_element_type=f32)[:8] for i in range(LOAD)]
        for slot, term in enumerate(terms, first):
            turned_ref[slot] = held_ref[slot].T
            if slot < cover:
                total_ref[slot] = term
            else:
                total_ref[cols_ref[0, 0, slot]] += jnp.where(slot < count, term, 0.0)
                sort(slot)

    for place in range(len(large)):
        if place * LOAD < cover:
            add(place)
        else:
            if_live(place, functools.partial(add, place))
    for place in range(cover):
        sent_ref[vectors + place : vectors + place + 1] = total_ref[place, :1]


def load(count, rows, cols, start_block, tiles, cover):
    slots, width = tiles.shape[0], tiles.shape[2]
    vectors = start_block.shape[0]
    places = [pltpu.SMEM(array.shape, jnp.int32) for array in (count, rows, cols)]
    places.append(pltpu.SMEM((2, slots - cover + 1), jnp.int32))
    sent = jax.ShapeDtypeStruct((vectors + cover + EXTRA, width), f32)
    operands = [count] + [pltpu.with_memory_space_constraint(array, pltpu.HBM) for array in (rows, cols, start_block, tiles)]
    return pl.pallas_call(
        load_kernel,
        out_shape=(pltpu.VMEM(tiles.shape, bf16), pltpu.VMEM(tiles.shape, bf16), sent, *places),
        in_specs=[HBM] * 5,
        out_specs=(VMEM, VMEM, VMEM, SMEM, SMEM, SMEM, SMEM),
        scratch_shapes=[
            pltpu.VMEM(start_block.shape, f32),
            pltpu.VMEM((cover, 8, width), f32),
            pltpu.SemaphoreType.DMA((slots // LOAD,)),
            pltpu.SemaphoreType.DMA((4,)),
        ],
        compiler_params=pltpu.CompilerParams(vmem_limit_bytes=16 * 2**20),
    )(*operands)


def add_products(count_ref, take_ref, put_ref, source_ref, held_ref, total_ref):
    count, cover = count_ref[0, 0], total_ref.shape[0]

    def product(slot, take):
        return jnp.dot(source_ref[take], held_ref[slot], preferred_element_type=f32)

    for slot in range(cover):
        total_ref[slot] = product(slot, slot)

    def add(first, group):
        places, terms = [], []
        for offset in range(group):
            slot = first + offset
            term = product(slot, take_ref[0, 0, slot])
            places.append(put_ref[0, 0, slot])
            terms.append(jnp.where(slot < count, term, 0.0))
        for place, term in zip(places, terms):
            total_ref[place] += term

    in_steps(cover, count, add)


def in_steps(first, end, add):
    large = (end - first + GROUP // 2 - 1) // GROUP
    after = first + large * GROUP
    lax.fori_loop(0, large, lambda index, _: add(first + index * GROUP, GROUP), None)
    small = jnp.maximum(end - after + SMALL - 1, 0) // SMALL
    lax.fori_loop(0, small, lambda index, _: add(after + index * SMALL, SMALL), None)


def add_side(side, sorted_ref, take_ref, put_ref, held_ref, source, total_ref, place, first):
    core, cover = lax.rem(lax.axis_index("row"), 2), take_ref.shape[2] + 1 - sorted_ref.shape[1]
    number = sorted_ref[side, sorted_ref.shape[1] - 1]

    def product(slot, take):
        return jnp.dot(source(take), held_ref[slot], preferred_element_type=f32)

    for index in range(cover // 2):
        slot = 2 * index + (core if side == 0 else 1 - core)
        term = product(slot, slot)
        if first:
            total_ref[place(slot)] = term
        else:
            total_ref[place(slot)] += term

    def add(start, group):
        places, terms = [], []
        for offset in range(group):
            index = start + offset
            slot = jnp.where(index < number, sorted_ref[side, index], 0)
            places.append(place(put_ref[0, 0, slot]))
            terms.append(jnp.where(index < number, product(slot, take_ref[0, 0, slot]), 0.0))
        for into, term in zip(places, terms):
            total_ref[into] += term

    in_steps(0, number, add)


def first_kernel(
    down, count_ref, take_ref, put_ref, mine_ref, theirs_ref, held_ref, out_ref, scale_ref,
    source_ref, total_ref,
):
    cover, width = total_ref.shape[0], total_ref.shape[2]
    half = width // 2
    vectors = (out_ref.shape[1] - EXTRA) // 2
    position = lax.axis_index("row")
    core = lax.rem(position, 2)
    degrees, top = jnp.zeros((cover, width), f32), None
    for place in range(cover // 2):
        degrees += mine_ref[place, vectors : vectors + cover] + theirs_ref[place, vectors : vectors + cover]
        larger = jnp.maximum(mine_ref[place, vectors + cover :], theirs_ref[place, vectors + cover :])
        top = larger if top is None else jnp.maximum(top, larger)
    scales = lax.rsqrt(degrees)
    scales = scales * (1.5 - 0.5 * degrees * scales * scales)
    index = lax.broadcasted_iota(jnp.int32, scales.shape, 0)
    scale_ref[...] = jnp.sum(jnp.where(index == position, scales, 0.0), axis=0, keepdims=True)
    for place in range(cover // 2):
        for other, ref in ((0, mine_ref), (1, theirs_ref)):
            odd = jnp.where(core == 1, 1 - other, other)
            scale = jnp.where(odd == 1, scales[2 * place + 1 : 2 * place + 2], scales[2 * place : 2 * place + 1])
            factor = scale * down * jnp.exp2(ref[place, vectors + cover :] - top)[:1]
            source_ref[2 * place + odd, :vectors] = (ref[place, :vectors] * factor).astype(bf16)
            source_ref[2 * place + odd, vectors:] = jnp.ones((16, width), bf16)
    add_products(count_ref, take_ref, put_ref, source_ref, held_ref, total_ref)
    row = lax.broadcasted_iota(jnp.int32, (EXTRA, half), 0)
    for part in range(2):
        lanes = pl.ds(part * half, half)
        out_ref[:, part * vectors : (part + 1) * vectors] = total_ref[:, :vectors, lanes]
    for place in range(cover):
        rest = top[:, :half]
        for part in range(2):
            high, low = halves_of(total_ref[place, vectors : vectors + EXTRA, part * half : (part + 1) * half])
            rest = jnp.where(row == part, high, jnp.where(row == 2 + part, low, rest))
        out_ref[place, 2 * vectors :] = rest


def first_product(count, take, put, mine, theirs, held, vectors, down):
    cover, width = mine.shape[0] * 2, mine.shape[2]
    return pl.pallas_call(
        functools.partial(first_kernel, down),
        out_shape=(
            jax.ShapeDtypeStruct((cover, 2 * vectors + EXTRA, width // 2), f32),
            jax.ShapeDtypeStruct((1, width), f32),
        ),
        in_specs=[SMEM, SMEM, SMEM, VMEM, VMEM, VMEM],
        out_specs=(VMEM, VMEM),
        scratch_shapes=[
            pltpu.VMEM((cover, vectors + 16, width), bf16),
            pltpu.VMEM((cover, vectors + 16, width), f32),
        ],
        compiler_params=pltpu.CompilerParams(vmem_limit_bytes=16 * 2**20),
    )(count, take, put, mine, theirs, held)


def forward_kernel(side, sorted_ref, take_ref, put_ref, source_ref, held_ref, *refs):
    total_ref, core = refs[-1], lax.rem(lax.axis_index("row"), 2)
    if side == 0:
        for index in range(total_ref.shape[0] // 2):
            total_ref[2 * index + 1 - core] = jnp.zeros(total_ref.shape[1:], f32)
    add_side(
        side, sorted_ref, take_ref, put_ref, held_ref, lambda take: source_ref[take // 2], total_ref, lambda p: p, side == 0
    )


def forward(side, places, take, put, source, held, total=None):
    shape = (source.shape[0] * 2, *source.shape[1:])
    return pl.pallas_call(
        functools.partial(forward_kernel, side),
        out_shape=jax.ShapeDtypeStruct(shape, f32),
        in_specs=[SMEM, SMEM, SMEM, VMEM, VMEM] + [VMEM] * side,
        out_specs=VMEM,
        input_output_aliases={5: 0} if side else {},
        compiler_params=pltpu.CompilerParams(vmem_limit_bytes=16 * 2**20),
    )(places, take, put, source, held, *([total] if side else []))


def backward_kernel(side, sorted_ref, take_ref, put_ref, source_ref, held_ref, total_ref):
    add_side(
        side, sorted_ref, take_ref, put_ref, held_ref, lambda take: source_ref[take], total_ref, lambda p: p // 2, True
    )


def backward(side, places, take, put, source, held):
    return pl.pallas_call(
        functools.partial(backward_kernel, side),
        out_shape=jax.ShapeDtypeStruct((source.shape[0] // 2, *source.shape[1:]), f32),
        in_specs=[SMEM, SMEM, SMEM, VMEM, VMEM],
        out_specs=VMEM,
        compiler_params=pltpu.CompilerParams(vmem_limit_bytes=16 * 2**20),
    )(places, take, put, source, held)


def on_device(start_block, tile_values, rows, cols, count):
    vectors, piece = start_block.shape
    tiles = tile_values[0, 0]
    slots, width = tiles.shape[0], tiles.shape[2]
    row_parts, col_parts = lax.axis_size("col"), lax.axis_size("row")
    chips = col_parts // 2
    same_core = [[2 * chip + core for chip in range(chips)] for core in range(2)]
    swap = [(index, index ^ 1) for index in range(col_parts)]

    nodes = piece * row_parts * col_parts
    longest = 2 * (slots - col_parts + 1) * width
    down = 2.0 ** math.floor(math.log2(60000.0 / (3.5 * math.sqrt(nodes * longest))))

    def over_chips(parts):
        return lax.all_to_all(parts, "row", 0, 0, axis_index_groups=same_core)

    def over_col(parts):
        return lax.all_to_all(parts, "col", 0, 0)

    def copies(block, parts):
        return jnp.broadcast_to(block[None], (parts, *block.shape))

    def other_core(block):
        return lax.ppermute(block, "row", swap)

    def add_parts(parts):
        return jnp.sum(parts.astype(f32), axis=0)

    held, turned, sent, count, rows, cols, places = load(count, rows, cols, start_block, tiles, col_parts)
    mine = over_chips(copies(sent.astype(f16), chips))
    theirs = other_core(mine)

    partial, col_scale = first_product(
        count, cols, rows, mine.astype(f32), theirs.astype(f32), turned, vectors, down
    )
    parts = over_col(partial.astype(f16)).astype(f32)
    rest = parts[:, 2 * vectors :]
    wide = [jnp.concatenate([rest[:, 2 * i], rest[:, 2 * i + 1]], axis=1) for i in range(3)]
    row_inverse = 1.0 / jnp.sum(wide[0] + wide[1] * (1.0 / FINE), axis=0)
    exponent = jnp.max(wide[2], axis=0)
    factors = jnp.exp2(wide[2] - exponent)[:, None]
    whole = jnp.concatenate([parts[:, :vectors], parts[:, vectors : 2 * vectors]], axis=2)
    mixed = add_parts(whole * factors)

    previous = current = None
    for index in range(DEGREE):
        if index:
            mine = over_chips(copies((col_scale * down * current).astype(bf16), chips))
            theirs = other_core(mine)
            partial = forward(0, places, cols, rows, mine, turned)
            partial = forward(1, places, cols, rows, theirs, turned, partial)
            mixed = add_parts(over_col(partial.astype(f16)))
        weighted = (mixed * row_inverse).astype(bf16)
        gathered = over_col(copies(weighted, row_parts))
        given = other_core(backward(1, places, rows, cols, gathered, held).astype(f16))
        keep = backward(0, places, rows, cols, gathered, held)
        parts = over_chips((keep + given.astype(f32)).astype(f16))
        if index:
            parts, current, previous, exponent = lax.optimization_barrier((parts, current, previous, exponent))
        else:
            parts, sent, exponent, col_scale = lax.optimization_barrier((parts, sent, exponent, col_scale))
            current = sent[:vectors] * jnp.exp2(sent[vectors + col_parts] - exponent)
        following = (col_scale * (1.0 / down) * add_parts(parts) - filter_center * current) / filter_half
        if index:
            following = 2.0 * following - previous
        previous, current = current, following
    up = jnp.exp2(exponent)
    return current * up, previous * up


def solution(mesh):
    return jax.shard_map(
        on_device,
        mesh=mesh,
        in_specs=(
            P(None, ("col", "row")),
            P("row", "col", None, None, None),
            P("row", "col", None),
            P("row", "col", None),
            P("row", "col"),
        ),
        out_specs=(P(None, ("col", "row")), P(None, ("col", "row"))),
        check_vma=False,
    )
```
